32 devices in a mesh: chain: 4 (over z), cross: 4 (over y, x), real: 2 (over core).
Axes of the slice: x: 2, y: 2, z: 4, core: 2. Of those that a mesh axis runs over, the one named last changes fastest.
Arguments:
- velocity_u: float32 [32, 256, 512], P('real', 'chain', 'cross'), may hold values from -4 to 4
- velocity_w: float32 [32, 256, 512], P('real', 'chain', 'cross'), may hold values from -4 to 4
- stress_uu: float32 [32, 256, 512], P('real', 'chain', 'cross'), may hold values from -6 to 6
- stress_ww: float32 [32, 256, 512], P('real', 'chain', 'cross'), may hold values from -6 to 6
- stress_uw: float32 [32, 256, 512], P('real', 'chain', 'cross'), may hold values from -6 to 6
- basis: float32 [48, 256, 512], P('real', 'chain', 'cross'), may hold values from -0.875 to 0.875
- coefficients: float32 [2, 32, 48], replicated, may hold values from -5 to 5
Outputs:
- velocity_u_out: float32 [32, 256, 512], P('real', 'chain', 'cross')
- velocity_w_out: float32 [32, 256, 512], P('real', 'chain', 'cross')
- stress_uu_out: float32 [32, 256, 512], P('real', 'chain', 'cross')
- stress_ww_out: float32 [32, 256, 512], P('real', 'chain', 'cross')
- stress_uw_out: float32 [32, 256, 512], P('real', 'chain', 'cross')
The draws below stay inside these ranges and needn't reach their ends.
All inputs are finite; a program needn't handle non-finite values.
Results may differ from the reference program's by a relative error of at most 0.00022.
Values sent between devices are 32-bit elements; how exact they have to be, the bound alone decides.
A program may use at most 128 MiB of HBM per device.

```python
import jax
import jax.numpy as jnp
from jax import lax

MODES = 48
STEPS = 6
NX = 256
NY = 512
REALIZ = 32


def block_scale(stream_key, dims, split, low, largest):
    def one(position, blocks):
        steps = jax.random.uniform(jax.random.fold_in(jax.random.fold_in(stream_key, 6), position), (blocks,), jnp.float32, low / len(split), largest / len(split))
        return jnp.repeat(jnp.exp(steps), dims[position] // blocks).reshape((-1,) + (1,) * (len(dims) - position - 1))

    factor_of = one(*split[0])
    for cut in split[1:]:
        factor_of = factor_of * one(*cut)
    return factor_of


def scatter_about(rng, extent, width, most, pieces=(), kind=jnp.bfloat16):
    loudness = block_scale(rng, extent, pieces, -0.22, 0.18) if pieces else 1.0
    drawn = jax.random.normal(rng, extent, jnp.float32) * width * loudness
    return jnp.minimum(jnp.maximum(drawn, -most), most).astype(kind)


def setup_inputs(seed: int = 0) -> dict:
    splits = jax.random.split(jax.random.key(seed), 8)
    velocity_u = scatter_about(splits[0], (REALIZ, NX, NY), 0.3, 4.0, ((0, 2), (1, 4), (2, 4)), jnp.float32)
    velocity_w = scatter_about(splits[1], (REALIZ, NX, NY), 0.3, 4.0, ((0, 2), (1, 4), (2, 4)), jnp.float32)
    stress_uu = scatter_about(splits[2], (REALIZ, NX, NY), 1.0, 6.0, ((0, 2), (1, 4), (2, 4)), jnp.float32)
    stress_ww = scatter_about(splits[3], (REALIZ, NX, NY), 1.0, 6.0, ((0, 2), (1, 4), (2, 4)), jnp.float32)
    stress_uw = scatter_about(splits[4], (REALIZ, NX, NY), 1.0, 6.0, ((0, 2), (1, 4), (2, 4)), jnp.float32)
    basis = scatter_about(splits[5], (MODES, NX, NY), MODES ** -0.5, 0.875, ((0, 2), (1, 4), (2, 4)), jnp.float32)
    coefficients = scatter_about(splits[6], (2, REALIZ, MODES), 1.0, 5.0, (), jnp.float32)
    return {"velocity_u": velocity_u, "velocity_w": velocity_w, "stress_uu": stress_uu, "stress_ww": stress_ww, "stress_uw": stress_uw, "basis": basis, "coefficients": coefficients}


time_step = 0.8
damping = 0.8
gravity = 0.1
modulus_m = 1.8
modulus_l = 0.6
modulus_g = 0.6

def along_x(padded):
    return 0.5 * (padded[..., 2:, 1:-1] - padded[..., :-2, 1:-1])

def along_y(padded):
    return 0.5 * (padded[..., 1:-1, 2:] - padded[..., 1:-1, :-2])

def material(field_c, field_f):
    cohesion = 0.5 * jnp.exp(0.7 * jnp.tanh(0.5 * field_c))
    angle = 0.6 + 0.25 * jnp.tanh(field_f)
    return (cohesion, jnp.sin(angle), jnp.cos(angle))

def forces(padded):
    return jnp.stack([along_x(padded[0]) + along_y(padded[2]), along_x(padded[2]) + along_y(padded[1]) - gravity])

def update_stress(stress, moving, cohesion, sine, cosine):
    strain_uu = along_x(moving[0])
    strain_ww = along_y(moving[1])
    shear = along_y(moving[0]) + along_x(moving[1])
    trial_uu = stress[0] + time_step * (modulus_m * strain_uu + modulus_l * strain_ww)
    trial_ww = stress[1] + time_step * (modulus_l * strain_uu + modulus_m * strain_ww)
    trial_uw = stress[2] + time_step * modulus_g * shear
    middle = 0.5 * (trial_uu + trial_ww)
    deviator = 0.5 * (trial_uu - trial_ww)
    radius = jnp.sqrt(deviator * deviator + trial_uw * trial_uw)
    strength = cohesion * cosine
    limit = jnp.maximum(strength - middle * sine, 0.1 * strength)
    factor = limit / jnp.maximum(radius, limit)
    return jnp.stack([middle + factor * deviator, middle - factor * deviator, factor * trial_uw])

def reference(velocity_u, velocity_w, stress_uu, stress_ww, stress_uw, basis, coefficients):

    def one_realization(items):
        moving, stress, coef = items
        fields = jnp.einsum('fk,kxy->fxy', coef, basis, precision=lax.Precision.HIGHEST)
        cohesion, sine, cosine = material(fields[0], fields[1])
        for number in range(STEPS):
            padded = jnp.pad(stress, ((0, 0), (1, 1), (1, 1)))
            moving = damping * moving + time_step * forces(padded)
            beside_all = jnp.pad(moving, ((0, 0), (1, 1), (1, 1)))
            stress = update_stress(stress, beside_all, cohesion, sine, cosine)
        return (moving, stress)
    moving_all = jnp.stack([velocity_u, velocity_w], 1)
    stress_all = jnp.stack([stress_uu, stress_ww, stress_uw], 1)
    coef_all = jnp.transpose(coefficients, (1, 0, 2))
    moving, stress = lax.map(one_realization, (moving_all, stress_all, coef_all))
    return (moving[:, 0], moving[:, 1], stress[:, 0], stress[:, 1], stress[:, 2])
```

```python
import functools
import math

import jax
import jax.numpy as jnp
from jax import lax
from jax.experimental import pallas as pl
from jax.experimental.pallas import tpu as pltpu
from jax.sharding import PartitionSpec as P

STEPS = 6
time_step = 0.8
damping = 0.8
gravity = 0.1
modulus_m = 1.8
modulus_l = 0.6
modulus_g = 0.6

MESH = pl.DeviceIdType.MESH
LANES = 128
PART = 8
TOP = 8
PIECES = 4

SINE = [(math.sin(0.6), math.cos(0.6), -math.sin(0.6), -math.cos(0.6))[n % 4] * 0.25**n / math.factorial(n) for n in range(8)]
COSINE = [(math.cos(0.6), -math.sin(0.6), -math.cos(0.6), math.sin(0.6))[n % 4] * 0.25**n / math.factorial(n) for n in range(8)]


def horner(coefs, t):
    total = jnp.full_like(t, coefs[-1])
    for c in coefs[-2::-1]:
        total = total * t + c
    return total


def kernel(
    sizes, vu_in, vw_in, suu_in, sww_in, suw_in, basis_in, coef_in,
    vu_out, vw_out, suu_out, sww_out, suw_out,
    vu, vw, suu, sww, suw, strength, sine, basis, panel,
    xsend, xrecv, ysend, yrecv,
    xs_sem, xr_sem, ys_sem, yr_sem, bs_sem, br_sem, own_sem,
):
    n_chain, n_cross, n_real, cells_x, cells_y, realiz, modes = sizes
    slabs = cells_x // PART
    last = slabs
    rows = cells_y // PIECES
    ci, xi, ri = lax.axis_index("chain"), lax.axis_index("cross"), lax.axis_index("real")
    has = {
        ("chain", 0): ci > 0, ("chain", 1): ci < n_chain - 1,
        ("cross", 0): xi > 0, ("cross", 1): xi < n_cross - 1,
    }
    beside = {
        ("chain", 0): ci - 1, ("chain", 1): ci + 1,
        ("cross", 0): xi - 1, ("cross", 1): xi + 1,
    }

    xrecv[...] = jnp.zeros_like(xrecv)
    yrecv[...] = jnp.zeros_like(yrecv)

    barrier = pltpu.get_barrier_semaphore()
    for key in has:
        @pl.when(has[key])
        def _(key=key):
            pl.semaphore_signal(barrier, inc=1, device_id={key[0]: beside[key]}, device_id_type=MESH)
    for d in range(1, n_real):
        pl.semaphore_signal(barrier, inc=1, device_id={"real": lax.rem(ri + d, n_real)}, device_id_type=MESH)
    greeted = n_real - 1
    for key in has:
        greeted = greeted + has[key].astype(jnp.int32)
    pl.semaphore_wait(barrier, greeted)

    block = basis_in.shape[0]
    place = pl.ds(pl.multiple_of(ri * block, 8), block)
    sends = []
    for d in range(1, n_real):
        copy = pltpu.make_async_remote_copy(
            basis_in, basis.at[place], bs_sem.at[d - 1], br_sem.at[d - 1],
            device_id={"real": lax.rem(ri + d, n_real)}, device_id_type=MESH)
        copy.start()
        sends.append(copy)
    own = pltpu.make_async_copy(basis_in, basis.at[place], own_sem)
    own.start()

    slot_of = lax.broadcasted_iota(jnp.int32, (rows, LANES), 1) % PART

    def x_copy(side, slot):
        return pltpu.make_async_remote_copy(
            xsend.at[side, slot], xrecv.at[1 - side, slot], xs_sem.at[side, slot], xr_sem.at[1 - side, slot],
            device_id={"chain": beside[("chain", side)]}, device_id_type=MESH)

    def y_copy(side, slot):
        return pltpu.make_async_remote_copy(
            ysend.at[side, slot], yrecv.at[1 - side, slot], ys_sem.at[side, slot], yr_sem.at[1 - side, slot],
            device_id={"cross": beside[("cross", side)]}, device_id_type=MESH)

    def send_x(slot, fields):
        for side in range(2):
            slab = (1, last)[side]
            packed = jnp.zeros((rows, LANES), jnp.float32)
            for j in range(2 * PIECES):
                part = fields[j // PIECES][slab, pl.ds(TOP + (j % PIECES) * rows, rows), :]
                shift = (j - (0, PART - 1)[side]) % LANES
                packed = jnp.where(slot_of == j, pltpu.roll(part, shift, 1) if shift else part, packed)
            xsend[side, slot] = packed

            @pl.when(has[("chain", side)])
            def _(side=side):
                x_copy(side, slot).start()

    def send_y(slot, fields):
        for side in range(2):
            row = (TOP, TOP + cells_y - 1)[side]
            for f in range(2):
                for i in range(slabs):
                    ysend[side, slot, pl.ds(f * slabs + i, 1), :] = fields[f][1 + i, pl.ds(row, 1), :]

            @pl.when(has[("cross", side)])
            def _(side=side):
                y_copy(side, slot).start()

    def receive_x(slot, fields):
        for side in range(2):
            @pl.when(has[("chain", side)])
            def _(side=side):
                x_copy(side, slot).wait_send()
                pltpu.make_async_remote_copy(
                    xsend.at[1 - side, slot], xrecv.at[side, slot], xs_sem.at[1 - side, slot], xr_sem.at[side, slot],
                    device_id={"chain": beside[("chain", side)]}, device_id_type=MESH).wait_recv()
        for side in range(2):
            got = xrecv[side, slot]
            slab, ghost = ((last, 0), (1, last + 1))[side]
            edge = (0, PART - 1)[side]
            for j in range(2 * PIECES):
                at = pl.ds(TOP + (j % PIECES) * rows, rows)
                mine = pltpu.roll(fields[j // PIECES][slab, at, :], (1, LANES - 1)[side], 1)
                shift = (edge - j) % LANES
                theirs = pltpu.roll(got, shift, 1) if shift else got
                fields[j // PIECES][ghost, at, :] = jnp.where(slot_of == edge, theirs, mine)

    def receive_y(slot, fields):
        for side in range(2):
            @pl.when(has[("cross", side)])
            def _(side=side):
                y_copy(side, slot).wait_send()
                pltpu.make_async_remote_copy(
                    ysend.at[1 - side, slot], yrecv.at[side, slot], ys_sem.at[1 - side, slot], yr_sem.at[side, slot],
                    device_id={"cross": beside[("cross", side)]}, device_id_type=MESH).wait_recv()
        for side in range(2):
            row = (TOP - 1, TOP + cells_y)[side]
            for f in range(2):
                for i in range(slabs):
                    fields[f][1 + i, pl.ds(row, 1), :] = yrecv[side, slot, pl.ds(f * slabs + i, 1), :]

    whole = pl.ds(TOP, cells_y)
    for source, field in ((suu_in, suu), (sww_in, sww), (suw_in, suw)):
        def turn(i, _, source=source, field=field):
            field[1 + i, whole, :] = source[pl.ds(i, LANES, stride=PART), :].T
            return 0
        lax.fori_loop(0, slabs, turn, 0)
    send_x(0, (suu, suw))
    send_y(0, (suw, sww))
    for source, field in ((vu_in, vu), (vw_in, vw)):
        def turn(i, _, source=source, field=field):
            field[1 + i, whole, :] = source[pl.ds(i, LANES, stride=PART), :].T
            return 0
        lax.fori_loop(0, slabs, turn, 0)

    own.wait()
    for copy in sends:
        copy.wait()
    weights = jnp.concatenate([coef_in[f, pl.ds(pl.multiple_of(ri * realiz, 8), realiz), :] for f in range(2)], axis=0)
    weights_high = weights.astype(jnp.bfloat16)
    weights_low = (weights - weights_high.astype(jnp.float32)).astype(jnp.bfloat16)
    both = jnp.concatenate([weights_high, weights_low], axis=0)
    half = 2 * realiz

    def material(i, _):
        for part in range(PART):
            values = basis[pl.ds(part * PART + i, modes, stride=cells_x), :]
            high = values.astype(jnp.bfloat16)
            low = (values - high.astype(jnp.float32)).astype(jnp.bfloat16)
            product = jnp.dot(both, jnp.concatenate([high, low], axis=1), preferred_element_type=jnp.float32)
            sums = product[:half, :cells_y] + (product[:half, cells_y:] + product[half:, :cells_y])
            panel[pl.ds(part, half, stride=PART), :] = sums
        field_c = panel[pl.ds(0, LANES), :].T
        field_f = panel[pl.ds(LANES, LANES), :].T
        t = jnp.tanh(field_f)
        cohesion = 0.5 * jnp.exp(0.7 * jnp.tanh(0.5 * field_c))
        strength[i] = cohesion * horner(COSINE, t)
        sine[i] = horner(SINE, t)
        return 0

    lax.fori_loop(0, slabs, material, 0)

    half_step = 0.5 * time_step

    def move(i, _):
        for p in range(PIECES):
            top = TOP + p * rows
            at, up, down = pl.ds(top, rows), pl.ds(top - 1, rows), pl.ds(top + 1, rows)
            pull_u = suu[i + 1, at, :] - suu[i - 1, at, :] + (suw[i, down, :] - suw[i, up, :])
            pull_w = suw[i + 1, at, :] - suw[i - 1, at, :] + (sww[i, down, :] - sww[i, up, :])
            vu[i, at, :] = damping * vu[i, at, :] + half_step * pull_u
            vw[i, at, :] = damping * vw[i, at, :] + (half_step * pull_w - time_step * gravity)
        return 0

    def strain(i, _):
        for p in range(PIECES):
            top = TOP + p * rows
            at, up, down = pl.ds(top, rows), pl.ds(top - 1, rows), pl.ds(top + 1, rows)
            strain_uu = vu[i + 1, at, :] - vu[i - 1, at, :]
            strain_ww = vw[i, down, :] - vw[i, up, :]
            shear = vu[i, down, :] - vu[i, up, :] + (vw[i + 1, at, :] - vw[i - 1, at, :])
            s_uu, s_ww = suu[i, at, :], sww[i, at, :]
            middle = 0.5 * (s_uu + s_ww) + (0.5 * half_step * (modulus_m + modulus_l)) * (strain_uu + strain_ww)
            deviator = 0.5 * (s_uu - s_ww) + (0.5 * half_step * (modulus_m - modulus_l)) * (strain_uu - strain_ww)
            trial_uw = suw[i, at, :] + (half_step * modulus_g) * shear
            k = strength[i - 1, pl.ds(p * rows, rows), :]
            limit = jnp.maximum(k - middle * sine[i - 1, pl.ds(p * rows, rows), :], 0.1 * k)
            factor = jnp.minimum(limit * lax.rsqrt(deviator * deviator + trial_uw * trial_uw), 1.0)
            deviator = factor * deviator
            suu[i, at, :] = middle + deviator
            sww[i, at, :] = middle - deviator
            suw[i, at, :] = factor * trial_uw
        return 0

    def step(number, _):
        receive_x(0, (suu, suw))
        receive_y(0, (suw, sww))
        lax.fori_loop(1, slabs + 1, move, 0)
        send_x(1, (vu, vw))
        send_y(1, (vu, vw))
        receive_x(1, (vu, vw))
        receive_y(1, (vu, vw))
        lax.fori_loop(1, slabs + 1, strain, 0)

        @pl.when(number < STEPS - 1)
        def _():
            send_x(0, (suu, suw))
            send_y(0, (suw, sww))
        return 0

    lax.fori_loop(0, STEPS, step, 0)

    for field, result in ((vu, vu_out), (vw, vw_out), (suu, suu_out), (sww, sww_out), (suw, suw_out)):
        def back(i, _, field=field, result=result):
            result[pl.ds(i, LANES, stride=PART), :] = field[1 + i, whole, :].T
            return 0
        lax.fori_loop(0, slabs, back, 0)


def shards(mesh, velocity_u, velocity_w, stress_uu, stress_ww, stress_uw, basis, coefficients):
    realiz, cells_x, cells_y = velocity_u.shape
    n_chain, n_cross, n_real = mesh.shape["chain"], mesh.shape["cross"], mesh.shape["real"]
    modes = basis.shape[0] * n_real
    slabs = cells_x // PART
    sizes = (n_chain, n_cross, n_real, cells_x, cells_y, realiz, modes)
    flat = lambda x: x.reshape(-1, cells_y)
    tall = cells_y + 2 * TOP
    f32 = jnp.float32
    vmem = pl.BlockSpec(memory_space=pltpu.VMEM)
    dma = pltpu.SemaphoreType.DMA
    results = pl.pallas_call(
        functools.partial(kernel, sizes),
        out_shape=[jax.ShapeDtypeStruct((realiz * cells_x, cells_y), f32)] * 5,
        in_specs=[vmem] * 7,
        out_specs=[vmem] * 5,
        scratch_shapes=[pltpu.VMEM((slabs + 2, tall, LANES), f32)] * 5 + [
            pltpu.VMEM((slabs, cells_y, LANES), f32),
            pltpu.VMEM((slabs, cells_y, LANES), f32),
            pltpu.VMEM((modes * cells_x, cells_y), f32),
            pltpu.VMEM((2 * LANES, cells_y), f32),
            pltpu.VMEM((2, 2, cells_y // PIECES, LANES), f32),
            pltpu.VMEM((2, 2, cells_y // PIECES, LANES), f32),
            pltpu.VMEM((2, 2, 2 * slabs, LANES), f32),
            pltpu.VMEM((2, 2, 2 * slabs, LANES), f32),
            dma((2, 2)), dma((2, 2)), dma((2, 2)), dma((2, 2)),
            dma((n_real - 1,)), dma((n_real - 1,)), dma,
        ],
        compiler_params=pltpu.CompilerParams(
            collective_id=0, has_side_effects=True, vmem_limit_bytes=40 * 2**20),
    )(*[flat(x) for x in (velocity_u, velocity_w, stress_uu, stress_ww, stress_uw, basis)], coefficients)
    return tuple(x.reshape(realiz, cells_x, cells_y) for x in results)


def solution(mesh):
    block = P("real", "chain", "cross")
    return jax.shard_map(
        functools.partial(shards, mesh),
        mesh=mesh,
        in_specs=(block,) * 6 + (P(),),
        out_specs=(block,) * 5,
        check_vma=False,
    )
```

```python
import functools
import math

import jax
import jax.numpy as jnp
from jax import lax
from jax.experimental import pallas as pl
from jax.experimental.pallas import tpu as pltpu
from jax.sharding import PartitionSpec as P

STEPS = 6
time_step = 0.8
damping = 0.8
gravity = 0.1
modulus_m = 1.8
modulus_l = 0.6
modulus_g = 0.6

MESH = pl.DeviceIdType.MESH
LANES = 128
PART = 8
TOP = 8
PIECES = 4

SINE = [(math.sin(0.6), math.cos(0.6), -math.sin(0.6), -math.cos(0.6))[n % 4] * 0.25**n / math.factorial(n) for n in range(8)]
COSINE = [(math.cos(0.6), -math.sin(0.6), -math.cos(0.6), math.sin(0.6))[n % 4] * 0.25**n / math.factorial(n) for n in range(8)]


def horner(coefs, t):
    total = jnp.full_like(t, coefs[-1])
    for c in coefs[-2::-1]:
        total = total * t + c
    return total


def kernel(
    sizes, vu_in, vw_in, suu_in, sww_in, suw_in, basis_in, coef_in,
    vu_out, vw_out, suu_out, sww_out, suw_out,
    vu, vw, suu, sww, suw, strength, sine, basis, panel, raw, coef,
    xsend, xrecv, ysend, yrecv, csend, crecv, turned, lines,
    xs_sem, xr_sem, ys_sem, yr_sem, cs_sem, cr_sem, bs_sem, br_sem, in_sem,
):
    n_chain, n_cross, n_real, cells_x, cells_y, realiz, modes = sizes
    slabs = cells_x // PART
    last = slabs
    rows = cells_y // PIECES
    ci, xi, ri = lax.axis_index("chain"), lax.axis_index("cross"), lax.axis_index("real")
    chain_has = (ci > 0, ci < n_chain - 1)
    cross_has = (xi > 0, xi < n_cross - 1)
    chain_to = (ci - 1, ci + 1)
    cross_to = (xi - 1, xi + 1)
    partners = [(chain_has[a], {"chain": chain_to[a]}) for a in range(2)]
    partners += [(cross_has[b], {"cross": cross_to[b]}) for b in range(2)]
    partners += [
        (jnp.logical_and(chain_has[a], cross_has[b]), {"chain": chain_to[a], "cross": cross_to[b]})
        for a in range(2) for b in range(2)]

    inputs = (suu_in, sww_in, suw_in, vu_in, vw_in)
    loads = [pltpu.make_async_copy(inputs[n], raw.at[n], in_sem.at[n]) for n in range(5)]
    for copy in loads:
        copy.start()
    coef_load = pltpu.make_async_copy(coef_in, coef, in_sem.at[5])
    coef_load.start()
    block = basis_in.shape[0]
    place = pl.ds(pl.multiple_of(ri * block, 8), block)
    own = pltpu.make_async_copy(basis_in, basis.at[place], in_sem.at[6])
    own.start()

    for buffer in (xrecv, yrecv, crecv, csend):
        buffer[...] = jnp.zeros_like(buffer)
    for field in (suw, sww):
        field[:, pl.ds(0, TOP), :] = jnp.zeros((slabs + 2, TOP, LANES), jnp.float32)
        field[:, pl.ds(TOP + cells_y, TOP), :] = jnp.zeros((slabs + 2, TOP, LANES), jnp.float32)

    barrier = pltpu.get_barrier_semaphore()
    greeted = n_real - 1
    for there, device in partners:
        @pl.when(there)
        def _(device=device):
            pl.semaphore_signal(barrier, inc=1, device_id=device, device_id_type=MESH)
        greeted = greeted + there.astype(jnp.int32)
    for d in range(1, n_real):
        pl.semaphore_signal(barrier, inc=1, device_id={"real": lax.rem(ri + d, n_real)}, device_id_type=MESH)
    pl.semaphore_wait(barrier, greeted)

    sends = []
    for d in range(1, n_real):
        copy = pltpu.make_async_remote_copy(
            basis_in, basis.at[place], bs_sem.at[d - 1], br_sem.at[d - 1],
            device_id={"real": lax.rem(ri + d, n_real)}, device_id_type=MESH)
        copy.start()
        sends.append(copy)

    slot_of = lax.broadcasted_iota(jnp.int32, (rows, LANES), 1) % PART
    slot_of_row = lax.broadcasted_iota(jnp.int32, (1, LANES), 1) % PART
    slot_of_line = lax.broadcasted_iota(jnp.int32, (slabs, LANES), 1) % PART
    line_of = lax.broadcasted_iota(jnp.int32, (slabs, LANES), 0)
    edges = (0, PART - 1)
    half_step = 0.5 * time_step
    signed = (half_step, -half_step)

    def copies(slot):
        found = []
        for n, (there, device) in enumerate(partners):
            if n < 2:
                source, target, out_sem, back_sem, mine, other = xsend, xrecv, xs_sem, xr_sem, (n,), (1 - n,)
            elif n < 4:
                source, target, out_sem, back_sem, mine, other = ysend, yrecv, ys_sem, yr_sem, (n - 2,), (3 - n,)
            else:
                p, q = (n - 4) // 2, (n - 4) % 2
                source, target, out_sem, back_sem, mine, other = csend, crecv, cs_sem, cr_sem, (p, q), (1 - p, 1 - q)
            make = lambda a, b: pltpu.make_async_remote_copy(
                source.at[(*a, slot)], target.at[(*b, slot)], out_sem.at[(*a, slot)], back_sem.at[(*b, slot)],
                device_id=device, device_id_type=MESH)
            found.append((there, make(mine, other), make(other, mine)))
        return found

    whole = pl.ds(TOP, cells_y)

    def piece(p):
        return pl.ds(TOP + p * rows, rows)

    def move(i, _):
        for p in range(PIECES):
            top = TOP + p * rows
            at, up, down = pl.ds(top, rows), pl.ds(top - 1, rows), pl.ds(top + 1, rows)
            pull_u = suu[i + 1, at, :] - suu[i - 1, at, :] + (suw[i, down, :] - suw[i, up, :])
            pull_w = suw[i + 1, at, :] - suw[i - 1, at, :] + (sww[i, down, :] - sww[i, up, :])
            vu[i, at, :] = damping * vu[i, at, :] + half_step * pull_u
            vw[i, at, :] = damping * vw[i, at, :] + (half_step * pull_w - time_step * gravity)
        return 0

    def strain(i, _):
        for p in range(PIECES):
            top = TOP + p * rows
            at, up, down = pl.ds(top, rows), pl.ds(top - 1, rows), pl.ds(top + 1, rows)
            strain_uu = vu[i + 1, at, :] - vu[i - 1, at, :]
            strain_ww = vw[i, down, :] - vw[i, up, :]
            shear = vu[i, down, :] - vu[i, up, :] + (vw[i + 1, at, :] - vw[i - 1, at, :])
            s_uu, s_ww = suu[i, at, :], sww[i, at, :]
            middle = 0.5 * (s_uu + s_ww) + (0.5 * half_step * (modulus_m + modulus_l)) * (strain_uu + strain_ww)
            deviator = 0.5 * (s_uu - s_ww) + (0.5 * half_step * (modulus_m - modulus_l)) * (strain_uu - strain_ww)
            trial_uw = suw[i, at, :] + (half_step * modulus_g) * shear
            k = strength[i - 1, pl.ds(p * rows, rows), :]
            limit = jnp.maximum(k - middle * sine[i - 1, pl.ds(p * rows, rows), :], 0.1 * k)
            factor = jnp.minimum(limit * lax.rsqrt(deviator * deviator + trial_uw * trial_uw), 1.0)
            deviator = factor * deviator
            suu[i, at, :] = middle + deviator
            sww[i, at, :] = middle - deviator
            suw[i, at, :] = factor * trial_uw
        return 0

    def prepare(slot):
        for t in range(2):
            for p in range(PIECES):
                for field in (suu, suw):
                    near = pltpu.roll(field[(last, 1)[t], piece(p), :], (1, LANES - 1)[t], 1)
                    field[(0, last + 1)[t], piece(p), :] = jnp.where(slot_of == edges[t], 0.0, near)
        lax.fori_loop(1, slabs + 1, move, 0)
        for t in range(2):
            slab = (1, last)[t]
            for group, fields in enumerate(((suu, suw), (vu, vw))):
                packed = jnp.zeros((rows, LANES), jnp.float32)
                for j in range(2 * PIECES):
                    part = fields[j // PIECES][slab, piece(j % PIECES), :]
                    shift = (j - edges[t]) % LANES
                    packed = jnp.where(slot_of == j, pltpu.roll(part, shift, 1) if shift else part, packed)
                xsend[t, slot, group] = packed
            row = (TOP, TOP + cells_y - 1)[t]
            for f, field in enumerate((suw, sww, vu, vw)):
                for i in range(slabs):
                    ysend[t, slot, pl.ds(f * slabs + i, 1), :] = field[1 + i, pl.ds(row, 1), :]
            for b in range(2):
                for k, field in enumerate((suu, suw, sww)):
                    csend[t, b, slot, pl.ds(k, 1), :] = field[slab, pl.ds((TOP, TOP + cells_y - 1)[b], 1), :]
        for there, copy, _ in copies(slot):
            @pl.when(there)
            def _(copy=copy):
                copy.start()

    def finish(slot):
        for there, copy, coming in copies(slot):
            @pl.when(there)
            def _(copy=copy, coming=coming):
                copy.wait_send()
                coming.wait_recv()
        for a in range(2):
            for b in range(2):
                turned[a, b] = pltpu.roll(crecv[a, b, slot], (LANES - PART + 1, PART - 1)[a], 1)
        for t in range(2):
            def got(f):
                return yrecv[t, slot, pl.ds(f * slabs, slabs), :]

            def mine(f):
                return ysend[t, slot, pl.ds(f * slabs, slabs), :]

            sg = signed[t]
            lines[pl.ds(0, slabs), :] = mine(2) - sg * got(0)
            lines[pl.ds(slabs, slabs), :] = mine(3) - sg * got(1)
            ghost_u = got(2) + sg * mine(0)
            ghost_w = got(3) + sg * mine(1)
            for a in range(2):
                here = jnp.logical_and(slot_of_line == edges[a], line_of == (0, slabs - 1)[a])
                ghost_u = ghost_u - jnp.where(here, signed[a] * turned[a, t, pl.ds(0, 1), :], 0.0)
                ghost_w = ghost_w - jnp.where(here, signed[a] * turned[a, t, pl.ds(1, 1), :], 0.0)
            there = cross_has[t].astype(jnp.float32)
            lines[pl.ds(2 * slabs, slabs), :] = ghost_u * there
            lines[pl.ds(3 * slabs, slabs), :] = ghost_w * there
            row, ghost = ((TOP, TOP - 1), (TOP + cells_y - 1, TOP + cells_y))[t]
            for f, (field, to) in enumerate(((vu, row), (vw, row), (vu, ghost), (vw, ghost))):
                for i in range(slabs):
                    field[1 + i, pl.ds(to, 1), :] = lines[pl.ds(f * slabs + i, 1), :]
        for t in range(2):
            slab, ghost, far = ((1, 0, last), (last, last + 1, 1))[t]
            sg = signed[t]
            there = chain_has[t].astype(jnp.float32)
            here = slot_of == edges[t]
            for p in range(PIECES):
                def theirs(group, f):
                    j = f * PIECES + p
                    shift = (edges[t] - j) % LANES
                    values = xrecv[t, slot, group]
                    return pltpu.roll(values, shift, 1) if shift else values

                at = piece(p)
                for f, (velocity, stress) in enumerate(((vu, suu), (vw, suw))):
                    now = velocity[slab, at, :]
                    velocity[slab, at, :] = jnp.where(here, now - sg * theirs(0, f), now)
                    outside = (theirs(1, f) + sg * stress[slab, at, :]) * there
                    near = pltpu.roll(velocity[far, at, :], (1, LANES - 1)[t], 1)
                    velocity[ghost, at, :] = jnp.where(here, outside, near)
            for b in range(2):
                row = pl.ds((TOP, TOP + cells_y - 1)[b], 1)
                for k, velocity in ((1, vu), (2, vw)):
                    fix = jnp.where(slot_of_row == edges[t], signed[b] * turned[t, b, pl.ds(k, 1), :], 0.0)
                    velocity[ghost, row, :] = velocity[ghost, row, :] - fix
        lax.fori_loop(1, slabs + 1, strain, 0)

    for n, field in enumerate((suu, sww, suw, vu, vw)):
        loads[n].wait()

        def turn(i, _, n=n, field=field):
            field[1 + i, whole, :] = raw[n, pl.ds(i, LANES, stride=PART), :].T
            return 0
        lax.fori_loop(0, slabs, turn, 0)
    prepare(0)

    coef_load.wait()
    own.wait()
    for copy in sends:
        copy.wait()
    weights = jnp.concatenate([coef[f, pl.ds(pl.multiple_of(ri * realiz, 8), realiz), :] for f in range(2)], axis=0)
    weights_high = weights.astype(jnp.bfloat16)
    weights_low = (weights - weights_high.astype(jnp.float32)).astype(jnp.bfloat16)
    both = jnp.concatenate([weights_high, weights_low], axis=0)
    half = 2 * realiz

    def material(i, _):
        for part in range(PART):
            values = basis[pl.ds(part * slabs + i, modes, stride=cells_x), :]
            high = values.astype(jnp.bfloat16)
            low = (values - high.astype(jnp.float32)).astype(jnp.bfloat16)
            product = jnp.dot(both, jnp.concatenate([high, low], axis=1), preferred_element_type=jnp.float32)
            sums = product[:half, :cells_y] + (product[:half, cells_y:] + product[half:, :cells_y])
            panel[pl.ds(part, half, stride=PART), :] = sums
        field_c = panel[pl.ds(0, LANES), :].T
        field_f = panel[pl.ds(LANES, LANES), :].T
        t = jnp.tanh(field_f)
        cohesion = 0.5 * jnp.exp(0.7 * jnp.tanh(0.5 * field_c))
        strength[i] = cohesion * horner(COSINE, t)
        sine[i] = horner(SINE, t)
        return 0

    lax.fori_loop(0, slabs, material, 0)

    def step(number, _):
        finish(number % 2)

        @pl.when(number < STEPS - 1)
        def _():
            prepare((number + 1) % 2)
        return 0

    lax.fori_loop(0, STEPS, step, 0)

    for field, result in ((vu, vu_out), (vw, vw_out), (suu, suu_out), (sww, sww_out), (suw, suw_out)):
        def back(i, _, field=field, result=result):
            result[pl.ds(i, LANES, stride=PART), :] = field[1 + i, whole, :].T
            return 0
        lax.fori_loop(0, slabs, back, 0)


def shards(mesh, velocity_u, velocity_w, stress_uu, stress_ww, stress_uw, basis, coefficients):
    realiz, cells_x, cells_y = velocity_u.shape
    n_chain, n_cross, n_real = mesh.shape["chain"], mesh.shape["cross"], mesh.shape["real"]
    modes = basis.shape[0] * n_real
    slabs = cells_x // PART
    sizes = (n_chain, n_cross, n_real, cells_x, cells_y, realiz, modes)
    flat = lambda x: x.reshape(-1, cells_y)
    tall = cells_y + 2 * TOP
    f32 = jnp.float32
    vmem = pl.BlockSpec(memory_space=pltpu.VMEM)
    dma = pltpu.SemaphoreType.DMA
    results = pl.pallas_call(
        functools.partial(kernel, sizes),
        out_shape=[jax.ShapeDtypeStruct((realiz * cells_x, cells_y), f32)] * 5,
        in_specs=[pl.BlockSpec(memory_space=pl.ANY)] * 7,
        out_specs=[vmem] * 5,
        scratch_shapes=[pltpu.VMEM((slabs + 2, tall, LANES), f32)] * 5 + [
            pltpu.VMEM((slabs, cells_y, LANES), f32),
            pltpu.VMEM((slabs, cells_y, LANES), f32),
            pltpu.VMEM((modes * cells_x, cells_y), f32),
            pltpu.VMEM((2 * LANES, cells_y), f32),
            pltpu.VMEM((5, realiz * cells_x, cells_y), f32),
            pltpu.VMEM(coefficients.shape, f32),
            pltpu.VMEM((2, 2, 2, cells_y // PIECES, LANES), f32),
            pltpu.VMEM((2, 2, 2, cells_y // PIECES, LANES), f32),
            pltpu.VMEM((2, 2, 4 * slabs, LANES), f32),
            pltpu.VMEM((2, 2, 4 * slabs, LANES), f32),
            pltpu.VMEM((2, 2, 2, 8, LANES), f32),
            pltpu.VMEM((2, 2, 2, 8, LANES), f32),
            pltpu.VMEM((2, 2, 8, LANES), f32),
            pltpu.VMEM((4 * slabs, LANES), f32),
            dma((2, 2)), dma((2, 2)), dma((2, 2)), dma((2, 2)), dma((2, 2, 2)), dma((2, 2, 2)),
            dma((n_real - 1,)), dma((n_real - 1,)), dma((7,)),
        ],
        compiler_params=pltpu.CompilerParams(
            collective_id=0, has_side_effects=True, vmem_limit_bytes=40 * 2**20),
    )(*[flat(x) for x in (velocity_u, velocity_w, stress_uu, stress_ww, stress_uw, basis)], coefficients)
    return tuple(x.reshape(realiz, cells_x, cells_y) for x in results)


def solution(mesh):
    block = P("real", "chain", "cross")
    return jax.shard_map(
        functools.partial(shards, mesh),
        mesh=mesh,
        in_specs=(block,) * 6 + (P(),),
        out_specs=(block,) * 5,
        check_vma=False,
    )
```

```python
import functools
import math

import jax
import jax.numpy as jnp
from jax import lax
from jax.experimental import pallas as pl
from jax.experimental.pallas import tpu as pltpu
from jax.sharding import PartitionSpec as P

STEPS = 6
time_step = 0.8
damping = 0.8
gravity = 0.1
modulus_m = 1.8
modulus_l = 0.6
modulus_g = 0.6

MESH = pl.DeviceIdType.MESH
LANES = 128
PART = 8
TOP = 8
PIECES = 4

SINE = [(math.sin(0.6), math.cos(0.6), -math.sin(0.6), -math.cos(0.6))[n % 4] * 0.25**n / math.factorial(n) for n in range(8)]
COSINE = [(math.cos(0.6), -math.sin(0.6), -math.cos(0.6), math.sin(0.6))[n % 4] * 0.25**n / math.factorial(n) for n in range(8)]


def horner(coefs, t):
    total = jnp.full_like(t, coefs[-1])
    for c in coefs[-2::-1]:
        total = total * t + c
    return total


def kernel(
    sizes, vu_in, vw_in, suu_in, sww_in, suw_in, basis_in, coef_in,
    vu, vw, suu, sww, suw, strength, sine, basis, panel, raw, coef,
    xsend, xrecv, ysend, yrecv, csend, crecv, turned, lines,
    xs_sem, xr_sem, ys_sem, yr_sem, cs_sem, cr_sem, bs_sem, br_sem, in_sem,
):
    n_chain, n_cross, n_real, cells_x, cells_y, realiz, modes = sizes
    slabs = cells_x // PART
    last = slabs
    rows = cells_y // PIECES
    ci, xi, ri = lax.axis_index("chain"), lax.axis_index("cross"), lax.axis_index("real")
    chain_has = (ci > 0, ci < n_chain - 1)
    cross_has = (xi > 0, xi < n_cross - 1)
    chain_to = (ci - 1, ci + 1)
    cross_to = (xi - 1, xi + 1)
    partners = [(chain_has[a], {"chain": chain_to[a]}) for a in range(2)]
    partners += [(cross_has[b], {"cross": cross_to[b]}) for b in range(2)]
    partners += [
        (jnp.logical_and(chain_has[a], cross_has[b]), {"chain": chain_to[a], "cross": cross_to[b]})
        for a in range(2) for b in range(2)]

    inputs = (suu_in, sww_in, suw_in, vu_in, vw_in)
    loads = [pltpu.make_async_copy(inputs[n], raw.at[n], in_sem.at[n]) for n in range(5)]
    for copy in loads:
        copy.start()
    coef_load = pltpu.make_async_copy(coef_in, coef, in_sem.at[5])
    coef_load.start()
    block = basis_in.shape[0]
    place = pl.ds(pl.multiple_of(ri * block, 8), block)
    own = pltpu.make_async_copy(basis_in, basis.at[place], in_sem.at[6])
    own.start()

    for buffer in (xrecv, yrecv, crecv, csend):
        buffer[...] = jnp.zeros_like(buffer)
    for field in (suw, sww):
        field[:, pl.ds(0, TOP), :] = jnp.zeros((slabs + 2, TOP, LANES), jnp.float32)
        field[:, pl.ds(TOP + cells_y, TOP), :] = jnp.zeros((slabs + 2, TOP, LANES), jnp.float32)

    barrier = pltpu.get_barrier_semaphore()
    greeted = n_real - 1
    for there, device in partners:
        @pl.when(there)
        def _(device=device):
            pl.semaphore_signal(barrier, inc=1, device_id=device, device_id_type=MESH)
        greeted = greeted + there.astype(jnp.int32)
    for d in range(1, n_real):
        pl.semaphore_signal(barrier, inc=1, device_id={"real": lax.rem(ri + d, n_real)}, device_id_type=MESH)
    pl.semaphore_wait(barrier, greeted)

    sends = []
    for d in range(1, n_real):
        copy = pltpu.make_async_remote_copy(
            basis_in, basis.at[place], bs_sem.at[d - 1], br_sem.at[d - 1],
            device_id={"real": lax.rem(ri + d, n_real)}, device_id_type=MESH)
        copy.start()
        sends.append(copy)

    slot_of = lax.broadcasted_iota(jnp.int32, (rows, LANES), 1) % PART
    slot_of_row = lax.broadcasted_iota(jnp.int32, (1, LANES), 1) % PART
    slot_of_line = lax.broadcasted_iota(jnp.int32, (slabs, LANES), 1) % PART
    line_of = lax.broadcasted_iota(jnp.int32, (slabs, LANES), 0)
    edges = (0, PART - 1)
    half_step = 0.5 * time_step
    signed = (half_step, -half_step)

    def copies(slot):
        found = []
        for n, (there, device) in enumerate(partners):
            if n < 2:
                source, target, out_sem, back_sem, mine, other = xsend, xrecv, xs_sem, xr_sem, (n,), (1 - n,)
            elif n < 4:
                source, target, out_sem, back_sem, mine, other = ysend, yrecv, ys_sem, yr_sem, (n - 2,), (3 - n,)
            else:
                p, q = (n - 4) // 2, (n - 4) % 2
                source, target, out_sem, back_sem, mine, other = csend, crecv, cs_sem, cr_sem, (p, q), (1 - p, 1 - q)
            make = lambda a, b: pltpu.make_async_remote_copy(
                source.at[(*a, slot)], target.at[(*b, slot)], out_sem.at[(*a, slot)], back_sem.at[(*b, slot)],
                device_id=device, device_id_type=MESH)
            found.append((there, make(mine, other), make(other, mine)))
        return found

    whole = pl.ds(TOP, cells_y)

    def piece(p):
        return pl.ds(TOP + p * rows, rows)

    def move(i, _):
        for p in range(PIECES):
            top = TOP + p * rows
            at, up, down = pl.ds(top, rows), pl.ds(top - 1, rows), pl.ds(top + 1, rows)
            pull_u = suu[i + 1, at, :] - suu[i - 1, at, :] + (suw[i, down, :] - suw[i, up, :])
            pull_w = suw[i + 1, at, :] - suw[i - 1, at, :] + (sww[i, down, :] - sww[i, up, :])
            vu[i, at, :] = damping * vu[i, at, :] + half_step * pull_u
            vw[i, at, :] = damping * vw[i, at, :] + (half_step * pull_w - time_step * gravity)
        return 0

    def strain(i, _):
        for p in range(PIECES):
            top = TOP + p * rows
            at, up, down = pl.ds(top, rows), pl.ds(top - 1, rows), pl.ds(top + 1, rows)
            strain_uu = vu[i + 1, at, :] - vu[i - 1, at, :]
            strain_ww = vw[i, down, :] - vw[i, up, :]
            shear = vu[i, down, :] - vu[i, up, :] + (vw[i + 1, at, :] - vw[i - 1, at, :])
            s_uu, s_ww = suu[i, at, :], sww[i, at, :]
            middle = 0.5 * (s_uu + s_ww) + (0.5 * half_step * (modulus_m + modulus_l)) * (strain_uu + strain_ww)
            deviator = 0.5 * (s_uu - s_ww) + (0.5 * half_step * (modulus_m - modulus_l)) * (strain_uu - strain_ww)
            trial_uw = suw[i, at, :] + (half_step * modulus_g) * shear
            k = strength[i - 1, pl.ds(p * rows, rows), :]
            limit = jnp.maximum(k - middle * sine[i - 1, pl.ds(p * rows, rows), :], 0.1 * k)
            factor = jnp.minimum(limit * lax.rsqrt(deviator * deviator + trial_uw * trial_uw), 1.0)
            deviator = factor * deviator
            suu[i, at, :] = middle + deviator
            sww[i, at, :] = middle - deviator
            suw[i, at, :] = factor * trial_uw
        return 0

    def prepare(slot):
        out = copies(slot)

        def start(those):
            for there, copy, _ in those:
                @pl.when(there)
                def _(copy=copy):
                    copy.start()

        for a in range(2):
            for b in range(2):
                for k, field in enumerate((suu, suw, sww)):
                    csend[a, b, slot, pl.ds(k, 1), :] = field[(1, last)[a], pl.ds((TOP, TOP + cells_y - 1)[b], 1), :]
        start(out[4:])
        for t in range(2):
            for p in range(PIECES):
                for field in (suu, suw):
                    near = pltpu.roll(field[(last, 1)[t], piece(p), :], (1, LANES - 1)[t], 1)
                    field[(0, last + 1)[t], piece(p), :] = jnp.where(slot_of == edges[t], 0.0, near)
        lax.fori_loop(1, slabs + 1, move, 0)
        for t in range(2):
            row = (TOP, TOP + cells_y - 1)[t]
            for f, field in enumerate((suw, sww, vu, vw)):
                for i in range(slabs):
                    ysend[t, slot, pl.ds(f * slabs + i, 1), :] = field[1 + i, pl.ds(row, 1), :]
        start(out[2:4])
        for t in range(2):
            slab = (1, last)[t]
            for group, fields in enumerate(((suu, suw), (vu, vw))):
                packed = jnp.zeros((rows, LANES), jnp.float32)
                for j in range(2 * PIECES):
                    part = fields[j // PIECES][slab, piece(j % PIECES), :]
                    shift = (j - edges[t]) % LANES
                    packed = jnp.where(slot_of == j, pltpu.roll(part, shift, 1) if shift else part, packed)
                xsend[t, slot, group] = packed
        start(out[:2])

    def finish(slot):
        for there, copy, coming in copies(slot):
            @pl.when(there)
            def _(copy=copy, coming=coming):
                copy.wait_send()
                coming.wait_recv()
        for a in range(2):
            for b in range(2):
                turned[a, b] = pltpu.roll(crecv[a, b, slot], (LANES - PART + 1, PART - 1)[a], 1)
        for t in range(2):
            def got(f):
                return yrecv[t, slot, pl.ds(f * slabs, slabs), :]

            def mine(f):
                return ysend[t, slot, pl.ds(f * slabs, slabs), :]

            sg = signed[t]
            lines[pl.ds(0, slabs), :] = mine(2) - sg * got(0)
            lines[pl.ds(slabs, slabs), :] = mine(3) - sg * got(1)
            ghost_u = got(2) + sg * mine(0)
            ghost_w = got(3) + sg * mine(1)
            for a in range(2):
                here = jnp.logical_and(slot_of_line == edges[a], line_of == (0, slabs - 1)[a])
                ghost_u = ghost_u - jnp.where(here, signed[a] * turned[a, t, pl.ds(0, 1), :], 0.0)
                ghost_w = ghost_w - jnp.where(here, signed[a] * turned[a, t, pl.ds(1, 1), :], 0.0)
            there = cross_has[t].astype(jnp.float32)
            lines[pl.ds(2 * slabs, slabs), :] = ghost_u * there
            lines[pl.ds(3 * slabs, slabs), :] = ghost_w * there
            row, ghost = ((TOP, TOP - 1), (TOP + cells_y - 1, TOP + cells_y))[t]
            for f, (field, to) in enumerate(((vu, row), (vw, row), (vu, ghost), (vw, ghost))):
                for i in range(slabs):
                    field[1 + i, pl.ds(to, 1), :] = lines[pl.ds(f * slabs + i, 1), :]
        for t in range(2):
            slab, ghost, far = ((1, 0, last), (last, last + 1, 1))[t]
            sg = signed[t]
            there = chain_has[t].astype(jnp.float32)
            here = slot_of == edges[t]
            for p in range(PIECES):
                def theirs(group, f):
                    j = f * PIECES + p
                    shift = (edges[t] - j) % LANES
                    values = xrecv[t, slot, group]
                    return pltpu.roll(values, shift, 1) if shift else values

                at = piece(p)
                for f, (velocity, stress) in enumerate(((vu, suu), (vw, suw))):
                    now = velocity[slab, at, :]
                    velocity[slab, at, :] = jnp.where(here, now - sg * theirs(0, f), now)
                    outside = (theirs(1, f) + sg * stress[slab, at, :]) * there
                    near = pltpu.roll(velocity[far, at, :], (1, LANES - 1)[t], 1)
                    velocity[ghost, at, :] = jnp.where(here, outside, near)
            for b in range(2):
                row = pl.ds((TOP, TOP + cells_y - 1)[b], 1)
                for k, velocity in ((1, vu), (2, vw)):
                    fix = jnp.where(slot_of_row == edges[t], signed[b] * turned[t, b, pl.ds(k, 1), :], 0.0)
                    velocity[ghost, row, :] = velocity[ghost, row, :] - fix
        lax.fori_loop(1, slabs + 1, strain, 0)

    for n, field in enumerate((suu, sww, suw, vu, vw)):
        loads[n].wait()
        for i in range(slabs):
            field[1 + i, whole, :] = raw[n, pl.ds(i, LANES, stride=slabs), :].T
    prepare(0)

    coef_load.wait()
    own.wait()
    for copy in sends:
        copy.wait()
    weights = jnp.concatenate([coef[f, pl.ds(pl.multiple_of(ri * realiz, 8), realiz), :] for f in range(2)], axis=0)
    weights_high = weights.astype(jnp.bfloat16)
    weights_low = (weights - weights_high.astype(jnp.float32)).astype(jnp.bfloat16)
    both = jnp.concatenate([weights_high, weights_low], axis=0)
    half = 2 * realiz

    def material(i, _):
        for part in range(PART):
            values = basis[pl.ds(part * slabs + i, modes, stride=cells_x), :]
            high = values.astype(jnp.bfloat16)
            low = (values - high.astype(jnp.float32)).astype(jnp.bfloat16)
            product = jnp.dot(both, jnp.concatenate([high, low], axis=1), preferred_element_type=jnp.float32)
            sums = product[:half, :cells_y] + (product[:half, cells_y:] + product[half:, :cells_y])
            panel[pl.ds(part, half, stride=PART), :] = sums
        field_c = panel[pl.ds(0, LANES), :].T
        field_f = panel[pl.ds(LANES, LANES), :].T
        t = jnp.tanh(field_f)
        cohesion = 0.5 * jnp.exp(0.7 * jnp.tanh(0.5 * field_c))
        strength[i] = cohesion * horner(COSINE, t)
        sine[i] = horner(SINE, t)
        return 0

    lax.fori_loop(0, slabs, material, 0)

    def step(number, _):
        finish(number % 2)

        @pl.when(number < STEPS - 1)
        def _():
            prepare((number + 1) % 2)
        return 0

    lax.fori_loop(0, STEPS, step, 0)


def turn_back(vu, vw, suu, sww, suw, vu_out, vw_out, suu_out, sww_out, suw_out, fields, held, load_sem, sem):
    cells_y, slabs = held.shape[2], vu.shape[0] - 2
    loads = [pltpu.make_async_copy(x, fields.at[n], load_sem.at[n]) for n, x in enumerate((vu, vw, suu, sww, suw))]
    for copy in loads:
        copy.start()
    copies = []
    for n, result in enumerate((vu_out, vw_out, suu_out, sww_out, suw_out)):
        loads[n].wait()
        for i in range(slabs):
            held[n, pl.ds(i, LANES, stride=slabs), :] = fields[n, 1 + i, pl.ds(TOP, cells_y), :].T
        copy = pltpu.make_async_copy(held.at[n], result, sem.at[n])
        copy.start()
        copies.append(copy)
    for copy in copies:
        copy.wait()


def shards(mesh, velocity_u, velocity_w, stress_uu, stress_ww, stress_uw, basis, coefficients):
    realiz, cells_x, cells_y = velocity_u.shape
    n_chain, n_cross, n_real = mesh.shape["chain"], mesh.shape["cross"], mesh.shape["real"]
    modes = basis.shape[0] * n_real
    slabs = cells_x // PART
    sizes = (n_chain, n_cross, n_real, cells_x, cells_y, realiz, modes)
    flat = lambda x: x.reshape(-1, cells_y)
    tall = cells_y + 2 * TOP
    f32 = jnp.float32
    vmem = pl.BlockSpec(memory_space=pltpu.VMEM)
    dma = pltpu.SemaphoreType.DMA
    turned = pl.pallas_call(
        functools.partial(kernel, sizes),
        out_shape=[jax.ShapeDtypeStruct((slabs + 2, tall, LANES), f32)] * 5,
        in_specs=[pl.BlockSpec(memory_space=pltpu.HBM)] * 7,
        out_specs=[vmem] * 5,
        scratch_shapes=[
            pltpu.VMEM((slabs, cells_y, LANES), f32),
            pltpu.VMEM((slabs, cells_y, LANES), f32),
            pltpu.VMEM((modes * cells_x, cells_y), f32),
            pltpu.VMEM((2 * LANES, cells_y), f32),
            pltpu.VMEM((5, realiz * cells_x, cells_y), f32),
            pltpu.VMEM(coefficients.shape, f32),
            pltpu.VMEM((2, 2, 2, cells_y // PIECES, LANES), f32),
            pltpu.VMEM((2, 2, 2, cells_y // PIECES, LANES), f32),
            pltpu.VMEM((2, 2, 4 * slabs, LANES), f32),
            pltpu.VMEM((2, 2, 4 * slabs, LANES), f32),
            pltpu.VMEM((2, 2, 2, 8, LANES), f32),
            pltpu.VMEM((2, 2, 2, 8, LANES), f32),
            pltpu.VMEM((2, 2, 8, LANES), f32),
            pltpu.VMEM((4 * slabs, LANES), f32),
            dma((2, 2)), dma((2, 2)), dma((2, 2)), dma((2, 2)), dma((2, 2, 2)), dma((2, 2, 2)),
            dma((n_real - 1,)), dma((n_real - 1,)), dma((7,)),
        ],
        compiler_params=pltpu.CompilerParams(
            collective_id=0, has_side_effects=True, vmem_limit_bytes=62 * 2**20),
    )(*[flat(x) for x in (velocity_u, velocity_w, stress_uu, stress_ww, stress_uw, basis)], coefficients)
    results = pl.pallas_call(
        turn_back,
        out_shape=[jax.ShapeDtypeStruct((realiz * cells_x, cells_y), f32)] * 5,
        in_specs=[pl.BlockSpec(memory_space=pltpu.HBM)] * 5,
        out_specs=[pl.BlockSpec(memory_space=pltpu.HBM)] * 5,
        scratch_shapes=[
            pltpu.VMEM((5, slabs + 2, tall, LANES), f32),
            pltpu.VMEM((5, realiz * cells_x, cells_y), f32), dma((5,)), dma((5,))],
        compiler_params=pltpu.CompilerParams(vmem_limit_bytes=62 * 2**20),
    )(*turned)
    return tuple(x.reshape(realiz, cells_x, cells_y) for x in results)


def solution(mesh):
    block = P("real", "chain", "cross")
    return jax.shard_map(
        functools.partial(shards, mesh),
        mesh=mesh,
        in_specs=(block,) * 6 + (P(),),
        out_specs=(block,) * 5,
        check_vma=False,
    )
```

```python
import functools
import math

import jax
import jax.numpy as jnp
from jax import lax
from jax.experimental import pallas as pl
from jax.experimental.pallas import tpu as pltpu
from jax.sharding import PartitionSpec as P

STEPS = 6
time_step = 0.8
damping = 0.8
gravity = 0.1
modulus_m = 1.8
modulus_l = 0.6
modulus_g = 0.6

MESH = pl.DeviceIdType.MESH
LANES = 128
PART = 8
TOP = 8
PIECES = 4

SINE = [(math.sin(0.6), math.cos(0.6), -math.sin(0.6), -math.cos(0.6))[n % 4] * 0.25**n / math.factorial(n) for n in range(8)]
COSINE = [(math.cos(0.6), -math.sin(0.6), -math.cos(0.6), math.sin(0.6))[n % 4] * 0.25**n / math.factorial(n) for n in range(8)]


def horner(coefs, t):
    total = jnp.full_like(t, coefs[-1])
    for c in coefs[-2::-1]:
        total = total * t + c
    return total


def kernel(
    sizes, vu_in, vw_in, suu_in, sww_in, suw_in, basis_in, coef_in,
    vu, vw, suu, sww, suw, strength, sine, basis, panel, raw, coef,
    xsend, xrecv, ysend, yrecv, csend, crecv, turned, lines,
    xs_sem, xr_sem, ys_sem, yr_sem, cs_sem, cr_sem, bs_sem, br_sem, in_sem,
):
    n_chain, n_cross, n_real, cells_x, cells_y, realiz, modes = sizes
    slabs = cells_x // PART
    last = slabs
    rows = cells_y // PIECES
    ci, xi, ri = lax.axis_index("chain"), lax.axis_index("cross"), lax.axis_index("real")
    chain_has = (ci > 0, ci < n_chain - 1)
    cross_has = (xi > 0, xi < n_cross - 1)
    chain_to = (ci - 1, ci + 1)
    cross_to = (xi - 1, xi + 1)
    partners = [(chain_has[a], {"chain": chain_to[a]}) for a in range(2)]
    partners += [(cross_has[b], {"cross": cross_to[b]}) for b in range(2)]
    partners += [
        (jnp.logical_and(chain_has[a], cross_has[b]), {"chain": chain_to[a], "cross": cross_to[b]})
        for a in range(2) for b in range(2)]

    inputs = (suu_in, sww_in, suw_in, vu_in, vw_in)
    loads = [pltpu.make_async_copy(inputs[n], raw.at[n], in_sem.at[n]) for n in range(5)]
    for copy in loads:
        copy.start()
    coef_load = pltpu.make_async_copy(coef_in, coef, in_sem.at[5])
    coef_load.start()
    block = basis_in.shape[0]
    place = pl.ds(pl.multiple_of(ri * block, 8), block)
    own = pltpu.make_async_copy(basis_in, basis.at[place], in_sem.at[6])
    own.start()

    for buffer in (xrecv, yrecv, crecv, csend):
        buffer[...] = jnp.zeros_like(buffer)
    for field in (suw, sww):
        field[:, pl.ds(0, TOP), :] = jnp.zeros((slabs + 2, TOP, LANES), jnp.float32)
        field[:, pl.ds(TOP + cells_y, TOP), :] = jnp.zeros((slabs + 2, TOP, LANES), jnp.float32)

    barrier = pltpu.get_barrier_semaphore()
    greeted = n_real - 1
    for there, device in partners:
        @pl.when(there)
        def _(device=device):
            pl.semaphore_signal(barrier, inc=1, device_id=device, device_id_type=MESH)
        greeted = greeted + there.astype(jnp.int32)
    for d in range(1, n_real):
        pl.semaphore_signal(barrier, inc=1, device_id={"real": lax.rem(ri + d, n_real)}, device_id_type=MESH)
    pl.semaphore_wait(barrier, greeted)

    sends = []
    for d in range(1, n_real):
        copy = pltpu.make_async_remote_copy(
            basis_in, basis.at[place], bs_sem.at[d - 1], br_sem.at[d - 1],
            device_id={"real": lax.rem(ri + d, n_real)}, device_id_type=MESH)
        copy.start()
        sends.append(copy)

    slot_of = lax.broadcasted_iota(jnp.int32, (rows, LANES), 1) % PART
    slot_of_row = lax.broadcasted_iota(jnp.int32, (1, LANES), 1) % PART
    slot_of_line = lax.broadcasted_iota(jnp.int32, (slabs, LANES), 1) % PART
    line_of = lax.broadcasted_iota(jnp.int32, (slabs, LANES), 0)
    edges = (0, PART - 1)
    half_step = 0.5 * time_step
    signed = (half_step, -half_step)

    def copies(slot):
        found = []
        for n, (there, device) in enumerate(partners):
            if n < 2:
                source, target, out_sem, back_sem, mine, other = xsend, xrecv, xs_sem, xr_sem, (n,), (1 - n,)
            elif n < 4:
                source, target, out_sem, back_sem, mine, other = ysend, yrecv, ys_sem, yr_sem, (n - 2,), (3 - n,)
            else:
                p, q = (n - 4) // 2, (n - 4) % 2
                source, target, out_sem, back_sem, mine, other = csend, crecv, cs_sem, cr_sem, (p, q), (1 - p, 1 - q)
            make = lambda a, b: pltpu.make_async_remote_copy(
                source.at[(*a, slot)], target.at[(*b, slot)], out_sem.at[(*a, slot)], back_sem.at[(*b, slot)],
                device_id=device, device_id_type=MESH)
            found.append((there, make(mine, other), make(other, mine)))
        return found

    whole = pl.ds(TOP, cells_y)

    def piece(p):
        return pl.ds(TOP + p * rows, rows)

    def move(i, _):
        for p in range(PIECES):
            top = TOP + p * rows
            at, up, down = pl.ds(top, rows), pl.ds(top - 1, rows), pl.ds(top + 1, rows)
            pull_u = suu[i + 1, at, :] - suu[i - 1, at, :] + (suw[i, down, :] - suw[i, up, :])
            pull_w = suw[i + 1, at, :] - suw[i - 1, at, :] + (sww[i, down, :] - sww[i, up, :])
            vu[i, at, :] = damping * vu[i, at, :] + half_step * pull_u
            vw[i, at, :] = damping * vw[i, at, :] + (half_step * pull_w - time_step * gravity)
        return 0

    def strain(i, pieces):
        for first, count in pieces:
            top = TOP + first
            at, up, down = pl.ds(top, count), pl.ds(top - 1, count), pl.ds(top + 1, count)
            strain_uu = vu[i + 1, at, :] - vu[i - 1, at, :]
            strain_ww = vw[i, down, :] - vw[i, up, :]
            shear = vu[i, down, :] - vu[i, up, :] + (vw[i + 1, at, :] - vw[i - 1, at, :])
            s_uu, s_ww = suu[i, at, :], sww[i, at, :]
            middle = 0.5 * (s_uu + s_ww) + (0.5 * half_step * (modulus_m + modulus_l)) * (strain_uu + strain_ww)
            deviator = 0.5 * (s_uu - s_ww) + (0.5 * half_step * (modulus_m - modulus_l)) * (strain_uu - strain_ww)
            trial_uw = suw[i, at, :] + (half_step * modulus_g) * shear
            k = strength[i - 1, pl.ds(first, count), :]
            limit = jnp.maximum(k - middle * sine[i - 1, pl.ds(first, count), :], 0.1 * k)
            factor = jnp.minimum(limit * lax.rsqrt(deviator * deviator + trial_uw * trial_uw), 1.0)
            deviator = factor * deviator
            suu[i, at, :] = middle + deviator
            sww[i, at, :] = middle - deviator
            suw[i, at, :] = factor * trial_uw
        return 0

    margin = 8
    inner = [(y, min(rows, cells_y - margin - y)) for y in range(margin, cells_y - margin, rows)]
    outer = [(0, margin), (cells_y - margin, margin)]
    full = [(p * rows, rows) for p in range(PIECES)]

    def prepare(slot):
        out = copies(slot)

        def start(those):
            for there, copy, _ in those:
                @pl.when(there)
                def _(copy=copy):
                    copy.start()

        for a in range(2):
            for b in range(2):
                for k, field in enumerate((suu, suw, sww)):
                    csend[a, b, slot, pl.ds(k, 1), :] = field[(1, last)[a], pl.ds((TOP, TOP + cells_y - 1)[b], 1), :]
        start(out[4:])
        for t in range(2):
            for p in range(PIECES):
                for field in (suu, suw):
                    near = pltpu.roll(field[(last, 1)[t], piece(p), :], (1, LANES - 1)[t], 1)
                    field[(0, last + 1)[t], piece(p), :] = jnp.where(slot_of == edges[t], 0.0, near)
        lax.fori_loop(1, slabs + 1, move, 0)
        for t in range(2):
            row = (TOP, TOP + cells_y - 1)[t]
            for f, field in enumerate((suw, sww, vu, vw)):
                for i in range(slabs):
                    ysend[t, slot, pl.ds(f * slabs + i, 1), :] = field[1 + i, pl.ds(row, 1), :]
        start(out[2:4])
        for t in range(2):
            slab = (1, last)[t]
            for group, fields in enumerate(((suu, suw), (vu, vw))):
                packed = jnp.zeros((rows, LANES), jnp.float32)
                for j in range(2 * PIECES):
                    part = fields[j // PIECES][slab, piece(j % PIECES), :]
                    shift = (j - edges[t]) % LANES
                    packed = jnp.where(slot_of == j, pltpu.roll(part, shift, 1) if shift else part, packed)
                xsend[t, slot, group] = packed
        start(out[:2])

    def finish(slot):
        lax.fori_loop(3, slabs - 1, lambda i, _: strain(i, inner), 0)
        for there, copy, coming in copies(slot):
            @pl.when(there)
            def _(copy=copy, coming=coming):
                copy.wait_send()
                coming.wait_recv()
        for a in range(2):
            for b in range(2):
                turned[a, b] = pltpu.roll(crecv[a, b, slot], (LANES - PART + 1, PART - 1)[a], 1)
        for t in range(2):
            def got(f):
                return yrecv[t, slot, pl.ds(f * slabs, slabs), :]

            def mine(f):
                return ysend[t, slot, pl.ds(f * slabs, slabs), :]

            sg = signed[t]
            lines[pl.ds(0, slabs), :] = mine(2) - sg * got(0)
            lines[pl.ds(slabs, slabs), :] = mine(3) - sg * got(1)
            ghost_u = got(2) + sg * mine(0)
            ghost_w = got(3) + sg * mine(1)
            for a in range(2):
                here = jnp.logical_and(slot_of_line == edges[a], line_of == (0, slabs - 1)[a])
                ghost_u = ghost_u - jnp.where(here, signed[a] * turned[a, t, pl.ds(0, 1), :], 0.0)
                ghost_w = ghost_w - jnp.where(here, signed[a] * turned[a, t, pl.ds(1, 1), :], 0.0)
            there = cross_has[t].astype(jnp.float32)
            lines[pl.ds(2 * slabs, slabs), :] = ghost_u * there
            lines[pl.ds(3 * slabs, slabs), :] = ghost_w * there
            row, ghost = ((TOP, TOP - 1), (TOP + cells_y - 1, TOP + cells_y))[t]
            for f, (field, to) in enumerate(((vu, row), (vw, row), (vu, ghost), (vw, ghost))):
                for i in range(slabs):
                    field[1 + i, pl.ds(to, 1), :] = lines[pl.ds(f * slabs + i, 1), :]
        for t in range(2):
            slab, ghost, far = ((1, 0, last), (last, last + 1, 1))[t]
            sg = signed[t]
            there = chain_has[t].astype(jnp.float32)
            here = slot_of == edges[t]
            for p in range(PIECES):
                def theirs(group, f):
                    j = f * PIECES + p
                    shift = (edges[t] - j) % LANES
                    values = xrecv[t, slot, group]
                    return pltpu.roll(values, shift, 1) if shift else values

                at = piece(p)
                for f, (velocity, stress) in enumerate(((vu, suu), (vw, suw))):
                    now = velocity[slab, at, :]
                    velocity[slab, at, :] = jnp.where(here, now - sg * theirs(0, f), now)
                    outside = (theirs(1, f) + sg * stress[slab, at, :]) * there
                    near = pltpu.roll(velocity[far, at, :], (1, LANES - 1)[t], 1)
                    velocity[ghost, at, :] = jnp.where(here, outside, near)
            for b in range(2):
                row = pl.ds((TOP, TOP + cells_y - 1)[b], 1)
                for k, velocity in ((1, vu), (2, vw)):
                    fix = jnp.where(slot_of_row == edges[t], signed[b] * turned[t, b, pl.ds(k, 1), :], 0.0)
                    velocity[ghost, row, :] = velocity[ghost, row, :] - fix
        lax.fori_loop(3, slabs - 1, lambda i, _: strain(i, outer), 0)
        lax.fori_loop(0, 4, lambda k, _: strain(1 + k + k // 2 * (slabs - 4), full), 0)

    for n, field in enumerate((suu, sww, suw, vu, vw)):
        loads[n].wait()
        for i in range(slabs):
            field[1 + i, whole, :] = raw[n, pl.ds(i, LANES, stride=slabs), :].T
    prepare(0)

    coef_load.wait()
    own.wait()
    for copy in sends:
        copy.wait()
    weights = jnp.concatenate([coef[f, pl.ds(pl.multiple_of(ri * realiz, 8), realiz), :] for f in range(2)], axis=0)
    weights_high = weights.astype(jnp.bfloat16)
    weights_low = (weights - weights_high.astype(jnp.float32)).astype(jnp.bfloat16)
    both = jnp.concatenate([weights_high, weights_low], axis=0)
    half = 2 * realiz

    def material(i, _):
        for part in range(PART):
            values = basis[pl.ds(part * slabs + i, modes, stride=cells_x), :]
            high = values.astype(jnp.bfloat16)
            low = (values - high.astype(jnp.float32)).astype(jnp.bfloat16)
            product = jnp.dot(both, jnp.concatenate([high, low], axis=1), preferred_element_type=jnp.float32)
            sums = product[:half, :cells_y] + (product[:half, cells_y:] + product[half:, :cells_y])
            panel[pl.ds(part, half, stride=PART), :] = sums
        field_c = panel[pl.ds(0, LANES), :].T
        field_f = panel[pl.ds(LANES, LANES), :].T
        t = jnp.tanh(field_f)
        cohesion = 0.5 * jnp.exp(0.7 * jnp.tanh(0.5 * field_c))
        strength[i] = cohesion * horner(COSINE, t)
        sine[i] = horner(SINE, t)
        return 0

    lax.fori_loop(0, slabs, material, 0)

    def step(number, _):
        finish(number % 2)

        @pl.when(number < STEPS - 1)
        def _():
            prepare((number + 1) % 2)
        return 0

    lax.fori_loop(0, STEPS, step, 0)


def turn_back(vu, vw, suu, sww, suw, vu_out, vw_out, suu_out, sww_out, suw_out, fields, held, load_sem, sem):
    cells_y, slabs = held.shape[2], vu.shape[0] - 2
    loads = [pltpu.make_async_copy(x, fields.at[n], load_sem.at[n]) for n, x in enumerate((vu, vw, suu, sww, suw))]
    for copy in loads:
        copy.start()
    copies = []
    for n, result in enumerate((vu_out, vw_out, suu_out, sww_out, suw_out)):
        loads[n].wait()
        for i in range(slabs):
            held[n, pl.ds(i, LANES, stride=slabs), :] = fields[n, 1 + i, pl.ds(TOP, cells_y), :].T
        copy = pltpu.make_async_copy(held.at[n], result, sem.at[n])
        copy.start()
        copies.append(copy)
    for copy in copies:
        copy.wait()


def shards(mesh, velocity_u, velocity_w, stress_uu, stress_ww, stress_uw, basis, coefficients):
    realiz, cells_x, cells_y = velocity_u.shape
    n_chain, n_cross, n_real = mesh.shape["chain"], mesh.shape["cross"], mesh.shape["real"]
    modes = basis.shape[0] * n_real
    slabs = cells_x // PART
    sizes = (n_chain, n_cross, n_real, cells_x, cells_y, realiz, modes)
    flat = lambda x: x.reshape(-1, cells_y)
    tall = cells_y + 2 * TOP
    f32 = jnp.float32
    vmem = pl.BlockSpec(memory_space=pltpu.VMEM)
    dma = pltpu.SemaphoreType.DMA
    turned = pl.pallas_call(
        functools.partial(kernel, sizes),
        out_shape=[jax.ShapeDtypeStruct((slabs + 2, tall, LANES), f32)] * 5,
        in_specs=[pl.BlockSpec(memory_space=pltpu.HBM)] * 7,
        out_specs=[vmem] * 5,
        scratch_shapes=[
            pltpu.VMEM((slabs, cells_y, LANES), f32),
            pltpu.VMEM((slabs, cells_y, LANES), f32),
            pltpu.VMEM((modes * cells_x, cells_y), f32),
            pltpu.VMEM((2 * LANES, cells_y), f32),
            pltpu.VMEM((5, realiz * cells_x, cells_y), f32),
            pltpu.VMEM(coefficients.shape, f32),
            pltpu.VMEM((2, 2, 2, cells_y // PIECES, LANES), f32),
            pltpu.VMEM((2, 2, 2, cells_y // PIECES, LANES), f32),
            pltpu.VMEM((2, 2, 4 * slabs, LANES), f32),
            pltpu.VMEM((2, 2, 4 * slabs, LANES), f32),
            pltpu.VMEM((2, 2, 2, 8, LANES), f32),
            pltpu.VMEM((2, 2, 2, 8, LANES), f32),
            pltpu.VMEM((2, 2, 8, LANES), f32),
            pltpu.VMEM((4 * slabs, LANES), f32),
            dma((2, 2)), dma((2, 2)), dma((2, 2)), dma((2, 2)), dma((2, 2, 2)), dma((2, 2, 2)),
            dma((n_real - 1,)), dma((n_real - 1,)), dma((7,)),
        ],
        compiler_params=pltpu.CompilerParams(
            collective_id=0, has_side_effects=True, vmem_limit_bytes=62 * 2**20),
    )(*[flat(x) for x in (velocity_u, velocity_w, stress_uu, stress_ww, stress_uw, basis)], coefficients)
    results = pl.pallas_call(
        turn_back,
        out_shape=[jax.ShapeDtypeStruct((realiz * cells_x, cells_y), f32)] * 5,
        in_specs=[pl.BlockSpec(memory_space=pltpu.HBM)] * 5,
        out_specs=[pl.BlockSpec(memory_space=pltpu.HBM)] * 5,
        scratch_shapes=[
            pltpu.VMEM((5, slabs + 2, tall, LANES), f32),
            pltpu.VMEM((5, realiz * cells_x, cells_y), f32), dma((5,)), dma((5,))],
        compiler_params=pltpu.CompilerParams(vmem_limit_bytes=62 * 2**20),
    )(*turned)
    return tuple(x.reshape(realiz, cells_x, cells_y) for x in results)


def solution(mesh):
    block = P("real", "chain", "cross")
    return jax.shard_map(
        functools.partial(shards, mesh),
        mesh=mesh,
        in_specs=(block,) * 6 + (P(),),
        out_specs=(block,) * 5,
        check_vma=False,
    )
```
